32 devices in a mesh: rev: 2 (over x), bin: 16 (over z, y, core).
Axes of the slice: x: 2, y: 2, z: 4, core: 2. Of those that a mesh axis runs over, the one named last changes fastest.
Arguments:
- snapshots: float32 [2, 512, 3, 6, 8, 128], P('rev', 'bin'), may hold values from -6 to 6
- phase_index: int32 [2, 512], P('rev', 'bin'), may hold values from 0 to 255, as said below
Outputs:
- stress_terms: float32 [4, 6, 256, 6, 8, 128], P(None, None, 'bin', 'rev')
- mean_velocity: float32 [3, 256, 6, 8, 128], P(None, 'bin', 'rev')
The draws below stay inside these ranges and needn't reach their ends.
Inputs may be any that keep to these rules, and one draw needn't show every extreme that they name: `phase_index`: the rows b * 32 to (b + 1) * 32 - 1 of a revolution shard name bins b * 16 to (b + 1) * 16 - 1 only, and each of these bins at least once.
All inputs are finite; a program needn't handle non-finite values.
Results may differ from the reference program's by a relative error of at most 0.00017.
Values sent between devices are 32-bit elements; how exact they have to be, the bound alone decides.
A program may use at most 64 MiB of HBM per device.

```python
import jax
import jax.numpy as jnp
from jax import lax

PHASES = 256
NY = 8
NZ = 128
PB_DEV = 16
SNAP_DEV = 32
SNAPS = 512
NX = 6
N_REV = 2
N_BIN = 16


def draw_phase_index(key, part):
    random_bins = jax.random.randint(jax.random.fold_in(key, 3), (N_REV, N_BIN, SNAP_DEV), 0, PB_DEV).astype(jnp.int32)
    position = jnp.arange(SNAP_DEV, dtype=jnp.int32)
    base = jnp.where(position[None, None, :] < PB_DEV, (position % PB_DEV)[None, None, :], random_bins)
    keys = jax.random.split(jax.random.fold_in(key, 7), N_REV * N_BIN)
    orders = jax.vmap(lambda single: jax.random.permutation(single, SNAP_DEV))(keys)
    orders = orders.reshape(N_REV, N_BIN, SNAP_DEV).astype(jnp.int32)
    local_bins = jnp.take_along_axis(base, orders, axis=2)
    first_bin = (jnp.arange(N_BIN, dtype=jnp.int32) * PB_DEV)[None, :, None]
    return (local_bins + first_bin).reshape(N_REV, N_BIN * SNAP_DEV).astype(jnp.int32)


def levels(rng, extent, cuts, low, largest):
    loudness = 1.0
    for axis_at, parts in cuts:
        draws = jax.random.uniform(jax.random.fold_in(jax.random.fold_in(rng, 6), axis_at), (parts,), jnp.float32, low / len(cuts), largest / len(cuts))
        loudness = loudness * jnp.repeat(jnp.exp(draws), extent[axis_at] // parts).reshape((-1,) + (1,) * (len(extent) - 1 - axis_at))
    return loudness


def normal_values(key, dims, spread, bound, shards=(), held_as=jnp.bfloat16):
    entries = jax.random.normal(key, dims, jnp.float32) * spread
    if len(shards) > 0:
        entries = levels(key, dims, shards, -0.22, 0.18) * entries
    return jnp.clip(entries, min=-bound, max=bound).astype(held_as)


def setup_inputs(seed: int = 0) -> dict:
    key_of = jax.random.split(jax.random.key(seed), 3)
    snapshots = normal_values(key_of[0], (N_REV, SNAPS, 3, NX, NY, NZ), 1.0, 6.0, ((0, 2), (1, 16)), jnp.float32)
    phase_index = draw_phase_index(jax.random.fold_in(key_of[2], 71), 0)
    return dict(snapshots=snapshots, phase_index=phase_index)


viscosity = 0.2
stress_pairs = ((0, 0), (0, 1), (0, 2), (1, 1), (1, 2), (2, 2))


def pair_index(first, second):
    low, high = min(first, second), max(first, second)
    return stress_pairs.index((low, high))


def moment_fields(frame):
    vel_x, vel_y, vel_z = frame[0], frame[1], frame[2]
    return jnp.stack([jnp.ones_like(vel_x), vel_x, vel_y, vel_z, vel_x * vel_x, vel_x * vel_y,
                      vel_x * vel_z, vel_y * vel_y, vel_y * vel_z, vel_z * vel_z])


def first_diff(field, axis):
    def shifted(amount):
        return jnp.roll(field, -amount, axis)
    return 0.75 * (shifted(1) - shifted(-1)) - 0.15 * (shifted(2) - shifted(-2)) + (shifted(3) - shifted(-3)) / 60.0


def second_diff(field, axis):
    def shifted(amount):
        return jnp.roll(field, -amount, axis)
    return (-49.0 / 18.0 * field + 1.5 * (shifted(1) + shifted(-1)) - 0.15 * (shifted(2) + shifted(-2))
            + (shifted(3) + shifted(-3)) / 90.0)


def reference(snapshots, phase_index):
    frames = snapshots.reshape((-1, 3, NX, NY, NZ))
    bin_list = phase_index.reshape(-1).astype(jnp.int32)

    def accumulate(running, entry):
        frame, which = entry
        return running.at[which].add(moment_fields(frame)), None

    sums, _ = lax.scan(accumulate, jnp.zeros((PHASES, 10, NX, NY, NZ), jnp.float32), (frames, bin_list))
    samples = sums[:, 0]
    velocity = [sums[:, 1 + comp] / samples for comp in range(3)]
    stresses = [sums[:, 4 + slot] / samples - velocity[pair[0]] * velocity[pair[1]]
                for slot, pair in enumerate(stress_pairs)]
    grad_u = [[first_diff(velocity[comp], 1 + dim) for dim in range(3)] for comp in range(3)]
    unsteady, convect, produce, diffuse = [], [], [], []
    for slot, pair in enumerate(stress_pairs):
        first, second = pair
        stress = stresses[slot]
        unsteady.append(first_diff(stress, 0))
        grads = [first_diff(stress, 1 + dim) for dim in range(3)]
        convect.append(velocity[0] * grads[0] + velocity[1] * grads[1] + velocity[2] * grads[2])
        summed = jnp.zeros_like(stress)
        for dim in range(3):
            summed = summed + stresses[pair_index(first, dim)] * grad_u[second][dim] + stresses[pair_index(second, dim)] * grad_u[first][dim]
        produce.append(-summed)
        diffuse.append(viscosity * (second_diff(stress, 1) + second_diff(stress, 2) + second_diff(stress, 3)))
    terms_all = jnp.stack([jnp.stack(unsteady), jnp.stack(convect), jnp.stack(produce), jnp.stack(diffuse)])
    return terms_all, jnp.stack(velocity)
```

```python
import functools

import jax
import jax.numpy as jnp
from jax import lax
from jax.experimental import pallas as pl
from jax.experimental.pallas import tpu as pltpu
from jax.sharding import PartitionSpec as P

PHASES = 256


viscosity = 0.2
stress_pairs = ((0, 0), (0, 1), (0, 2), (1, 1), (1, 2), (2, 2))


def padded_2(cells, sides, width):
    for axis, dim in sides:
        count = lax.axis_size(axis)
        head = lax.slice_in_dim(cells, 0, width, axis=dim)
        tail = lax.slice_in_dim(cells, cells.shape[dim] - width, cells.shape[dim], axis=dim)
        cells = jnp.concatenate(
            [
                lax.ppermute(tail, axis, [(i, (i + 1) % count) for i in range(count)]),
                cells,
                lax.ppermute(head, axis, [((i + 1) % count, i) for i in range(count)]),
            ],
            axis=dim,
        )
    return cells


def pair_index(first, second):
    low, high = (min(first, second), max(first, second))
    return stress_pairs.index((low, high))


def binned(frames, weights):
    vel_x, vel_y, vel_z = (frames[:, 0], frames[:, 1], frames[:, 2])
    stacked = jnp.stack(
        [
            jnp.ones_like(vel_x),
            vel_x,
            vel_y,
            vel_z,
            vel_x * vel_x,
            vel_x * vel_y,
            vel_x * vel_z,
            vel_y * vel_y,
            vel_y * vel_z,
            vel_z * vel_z,
        ],
        axis=1,
    )
    return jnp.einsum("ps,sfxyz->xfpyz", weights, stacked, precision=lax.Precision.HIGHEST)


def first_diff(shifted):
    return (
        0.75 * (shifted(1) - shifted(-1))
        - 0.15 * (shifted(2) - shifted(-2))
        + (shifted(3) - shifted(-3)) / 60.0
    )


def second_diff(shifted, centre):
    return (
        -49.0 / 18.0 * centre
        + 1.5 * (shifted(1) + shifted(-1))
        - 0.15 * (shifted(2) + shifted(-2))
        + (shifted(3) + shifted(-3)) / 90.0
    )


def finish_terms(owned):
    planes, bins_dev = (owned.shape[0], owned.shape[2])
    samples = owned[:, 0]
    velocity = [owned[:, 1 + comp] / samples for comp in range(3)]
    stresses = [
        owned[:, 4 + slot] / samples - velocity[pair[0]] * velocity[pair[1]]
        for slot, pair in enumerate(stress_pairs)
    ]
    fields = jnp.stack(velocity + stresses, axis=1)
    padded = padded_2(fields, (("rev", 0), ("bin", 2)), 3)

    def along(component, dim, centre):
        source = padded[:, component]
        if dim == 0:
            return lambda amount: source[3 + amount : 3 + amount + planes, 3 : 3 + bins_dev]
        if dim == 3:
            return lambda amount: source[3 : 3 + planes, 3 + amount : 3 + amount + bins_dev]
        return lambda amount: jnp.roll(centre, -amount, dim + 1)

    grad_u = [
        [first_diff(along(comp, dim, velocity[comp])) for dim in range(3)] for comp in range(3)
    ]
    unsteady, convect, produce, diffuse = ([], [], [], [])
    for slot, pair in enumerate(stress_pairs):
        first, second = pair
        stress = stresses[slot]
        unsteady.append(first_diff(along(3 + slot, 3, stress)))
        grads = [first_diff(along(3 + slot, dim, stress)) for dim in range(3)]
        convect.append(velocity[0] * grads[0] + velocity[1] * grads[1] + velocity[2] * grads[2])
        summed = jnp.zeros_like(stress)
        for dim in range(3):
            summed = (
                summed
                + stresses[pair_index(first, dim)] * grad_u[second][dim]
                + stresses[pair_index(second, dim)] * grad_u[first][dim]
            )
        produce.append(-summed)
        diffuse.append(
            viscosity
            * (
                second_diff(along(3 + slot, 0, stress), stress)
                + second_diff(along(3 + slot, 1, stress), stress)
                + second_diff(along(3 + slot, 2, stress), stress)
            )
        )
    terms_all = jnp.stack(
        [jnp.stack(unsteady), jnp.stack(convect), jnp.stack(produce), jnp.stack(diffuse)]
    )
    return (
        jnp.transpose(terms_all, (0, 1, 3, 2, 4, 5)),
        jnp.transpose(jnp.stack(velocity), (0, 2, 1, 3, 4)),
    )


def shards(snapshots, phase_index):
    frames = snapshots[0]
    bins_dev = PHASES // lax.axis_size("bin")
    local_bins = phase_index[0] - lax.axis_index("bin") * bins_dev
    exchanged = lax.all_to_all(frames, "rev", split_axis=2, concat_axis=0, tiled=True)
    all_bins = lax.all_gather(local_bins, "rev", axis=0, tiled=True)
    one_hot = (all_bins[None, :] == jnp.arange(bins_dev, dtype=jnp.int32)[:, None]).astype(
        jnp.float32
    )
    owned = binned(exchanged, one_hot)
    return finish_terms(owned)


MESH = pl.DeviceIdType.MESH
DEPTH = 2
GROUPS = 4


def turned(tile, amount, axis):
    size = tile.shape[axis]
    return pltpu.roll(tile, (-amount) % size, axis)


def both_diffs(tile, axis):
    plus = [turned(tile, s, axis) for s in (1, 2, 3)]
    minus = [turned(tile, -s, axis) for s in (1, 2, 3)]
    d1 = 0.75 * (plus[0] - minus[0]) - 0.15 * (plus[1] - minus[1]) + (plus[2] - minus[2]) * (1.0 / 60.0)
    d2 = (
        (-49.0 / 18.0) * tile
        + 1.5 * (plus[0] + minus[0])
        - 0.15 * (plus[1] + minus[1])
        + (plus[2] + minus[2]) * (1.0 / 90.0)
    )
    return d1, d2


def ring_kernel(
    sizes, snap, index, terms, mean,
    own, peer, heap, fields, held, held_mean, idx_own, idx_peer, idx_s, tab_v, tab_s, inv_v, inv_s,
    load_sem, small_sem, idx_sem, send_sem, recv_sem, halo_send, halo_recv, out_sem,
):
    snaps, nx, planes, bins, nbin = sizes
    rev, me = lax.axis_index("rev"), lax.axis_index("bin")
    left, right = lax.rem(me + nbin - 1, nbin), lax.rem(me + 1, nbin)
    other = 1 - rev

    whole = pltpu.make_async_copy(snap.at[0], own, load_sem.at[0])
    whole.start()
    barrier = pltpu.get_barrier_semaphore()
    for target in ((other, me), (rev, left), (rev, right)):
        pl.semaphore_signal(barrier, inc=1, device_id=target, device_id_type=MESH)
    idx_own[...] = jnp.full(idx_own.shape, -1, jnp.int32)
    idx_own[0:1, 0:snaps] = index[...] - me * bins
    pl.semaphore_wait(barrier, 3)

    copy_idx = pltpu.make_async_remote_copy(
        src_ref=idx_own, dst_ref=idx_peer, send_sem=idx_sem.at[0], recv_sem=idx_sem.at[1],
        device_id=(other, me), device_id_type=MESH,
    )
    copy_idx.start()
    sends = []
    for q in range(nx):
        plane = lax.rem(q + planes * other, nx)
        sends.append(
            pltpu.make_async_remote_copy(
                src_ref=snap.at[0, :, :, plane], dst_ref=peer.at[q],
                send_sem=send_sem.at[q], recv_sem=recv_sem.at[q],
                device_id=(other, me), device_id_type=MESH,
            )
        )
    for q in range(DEPTH):
        sends[q].start()

    copy_idx.wait()
    lane = lax.broadcasted_iota(jnp.int32, (1, 128), 1)
    row = jnp.where(lane < snaps, idx_own[0:1, :], pltpu.roll(idx_peer[0:1, :], snaps, 1))
    idx_own[1:2, :] = row
    to_s = pltpu.make_async_copy(idx_own, idx_s, small_sem.at[0])
    to_s.start()
    to_s.wait()

    def link(j, carry):
        prev, last, count = carry
        b = idx_s[1, j]
        prev = jnp.where((row == b) & (lane > j), j + 1, prev)
        hit = lane == b
        return prev, jnp.where(hit, j + 1, last), count + jnp.where(hit, 1.0, 0.0)

    zero_i = jnp.zeros((1, 128), jnp.int32)
    prev, last, count = lax.fori_loop(
        0, 2 * snaps, link, (zero_i, zero_i, jnp.zeros((1, 128), jnp.float32))
    )
    tab_v[...] = jnp.zeros(tab_v.shape, jnp.int32)
    tab_v[0:1, :] = prev
    tab_v[1:2, :] = last
    inv_v[...] = jnp.broadcast_to(1.0 / jnp.maximum(count, 1.0), inv_v.shape)
    to_t = pltpu.make_async_copy(tab_v, tab_s, small_sem.at[1])
    to_i = pltpu.make_async_copy(inv_v, inv_s, small_sem.at[2])
    to_t.start()
    to_i.start()
    zero = jnp.zeros(heap.shape[-2:], jnp.float32)
    for q in range(nx):
        for m in range(9):
            heap[q, 0, m] = zero
    to_t.wait()
    to_i.wait()
    whole.wait()

    def moments(vel):
        out = list(vel)
        for a, b in stress_pairs:
            out.append(vel[a] * vel[b])
        return out

    def add_own(k, carry):
        before = tab_s[0, k]
        for q in range(nx):
            plane = lax.rem(q + planes * rev, nx)
            values = moments([own[k, c, plane] for c in range(3)])
            for m in range(9):
                heap[q, k + 1, m] = heap[q, before, m] + values[m]
        return carry

    lax.fori_loop(0, snaps, add_own, 0)

    def add_peer(q):
        def body(k, carry):
            before = tab_s[0, k + snaps]
            values = moments([peer[q, k, c] for c in range(3)])
            for m in range(9):
                heap[q, k + snaps + 1, m] = heap[q, before, m] + values[m]
            return carry

        lax.fori_loop(0, snaps, body, 0)

        def finish(p, carry):
            at = tab_s[1, p]
            scale = inv_s[0, p]
            vel = [heap[q, at, c] * scale for c in range(3)]
            for c in range(3):
                fields[q, c, p + 3] = vel[c]
                if q < planes:
                    held_mean[c, p, q] = vel[c]
            for m, (a, b) in enumerate(stress_pairs):
                fields[q, 3 + m, p + 3] = heap[q, at, 3 + m] * scale - vel[a] * vel[b]
            return carry

        lax.fori_loop(0, bins, finish, 0)

    def in_plane(q):
        def body(p, carry):
            vel = [fields[q, c, p + 3] for c in range(3)]
            stress = [fields[q, 3 + m, p + 3] for m in range(6)]
            grad = []
            for c in range(3):
                grad.append([both_diffs(vel[c], 0)[0], both_diffs(vel[c], 1)[0]])
            for m, (a, b) in enumerate(stress_pairs):
                y1, y2 = both_diffs(stress[m], 0)
                z1, z2 = both_diffs(stress[m], 1)
                held[1, m, p, q] = vel[1] * y1 + vel[2] * z1
                held[3, m, p, q] = y2 + z2
                total = None
                for k in (1, 2):
                    part = stress[pair_index(a, k)] * grad[b][k - 1] + stress[pair_index(b, k)] * grad[a][k - 1]
                    total = part if total is None else total + part
                held[2, m, p, q] = total
            return carry

        lax.fori_loop(0, bins, body, 0)

    halos = []
    for q in range(planes):
        halos.append(
            (
                pltpu.make_async_remote_copy(
                    src_ref=fields.at[q, 3:9, 3:6], dst_ref=fields.at[q, 3:9, bins + 3 : bins + 6],
                    send_sem=halo_send.at[2 * q], recv_sem=halo_recv.at[2 * q],
                    device_id=(rev, left), device_id_type=MESH,
                ),
                pltpu.make_async_remote_copy(
                    src_ref=fields.at[q, 3:9, bins : bins + 3], dst_ref=fields.at[q, 3:9, 0:3],
                    send_sem=halo_send.at[2 * q + 1], recv_sem=halo_recv.at[2 * q + 1],
                    device_id=(rev, right), device_id_type=MESH,
                ),
            )
        )

    def in_phase(q):
        def body(p, carry):
            for m in range(6):
                f = lambda s: fields[q, 3 + m, p + 3 + s]
                held[0, m, p, q] = (
                    0.75 * (f(1) - f(-1)) - 0.15 * (f(2) - f(-2)) + (f(3) - f(-3)) * (1.0 / 60.0)
                )
            return carry

        lax.fori_loop(0, bins, body, 0)

    outs = []
    for q in range(nx):
        sends[q].wait()
        if q + DEPTH < nx:
            sends[q + DEPTH].start()
        add_peer(q)
        if q < planes:
            for halo in halos[q]:
                halo.start()
            in_plane(q)
        if 1 <= q <= planes:
            for halo in halos[q - 1]:
                halo.wait()
            in_phase(q - 1)
        if q == planes:
            out = pltpu.make_async_copy(held_mean, mean, out_sem.at[0])
            out.start()
            outs.append(out)
            out = pltpu.make_async_copy(held.at[0], terms.at[0], out_sem.at[1])
            out.start()
            outs.append(out)

    def across(tiles, q):
        f = lambda s: tiles[(q + s) % nx]
        d1 = 0.75 * (f(1) - f(-1)) - 0.15 * (f(2) - f(-2)) + (f(3) - f(-3)) * (1.0 / 60.0)
        d2 = (
            (-49.0 / 18.0) * f(0)
            + 1.5 * (f(1) + f(-1))
            - 0.15 * (f(2) + f(-2))
            + (f(3) + f(-3)) * (1.0 / 90.0)
        )
        return d1, d2

    def last_terms(p, carry):
        grad = []
        for c in range(3):
            tiles = [fields[q, c, p + 3] for q in range(nx)]
            grad.append([across(tiles, q)[0] for q in range(planes)])
        for m in range(6):
            tiles = [fields[q, 3 + m, p + 3] for q in range(nx)]
            for q in range(planes):
                d1, d2 = across(tiles, q)
                held[1, m, p, q] = held[1, m, p, q] + fields[q, 0, p + 3] * d1
                held[3, m, p, q] = viscosity * (held[3, m, p, q] + d2)
        for q in range(planes):
            stress = [fields[q, 3 + m, p + 3] for m in range(6)]
            for m, (a, b) in enumerate(stress_pairs):
                part = stress[pair_index(a, 0)] * grad[b][q] + stress[pair_index(b, 0)] * grad[a][q]
                held[2, m, p, q] = -(held[2, m, p, q] + part)
        return carry

    each = bins // GROUPS
    for g in range(GROUPS):
        lax.fori_loop(g * each, (g + 1) * each, last_terms, 0)
        out = pltpu.make_async_copy(
            held.at[1:4, :, g * each : (g + 1) * each],
            terms.at[1:4, :, g * each : (g + 1) * each],
            out_sem.at[2 + g],
        )
        out.start()
        outs.append(out)
    for out in outs:
        out.wait()


def paired_shards(snapshots, phase_index):
    _, snaps, _, nx, ny, nz = snapshots.shape
    nbin, nrev = lax.axis_size("bin"), lax.axis_size("rev")
    bins, planes = PHASES // nbin, nx // nrev
    sizes = (snaps, nx, planes, bins, nbin)
    f32, i32 = jnp.float32, jnp.int32
    vmem, dma = pltpu.VMEM, pltpu.SemaphoreType.DMA
    return pl.pallas_call(
        functools.partial(ring_kernel, sizes),
        out_shape=(
            jax.ShapeDtypeStruct((4, 6, bins, planes, ny, nz), f32),
            jax.ShapeDtypeStruct((3, bins, planes, ny, nz), f32),
        ),
        in_specs=[pl.BlockSpec(memory_space=pl.ANY), pl.BlockSpec(memory_space=pltpu.VMEM)],
        out_specs=[pl.BlockSpec(memory_space=pl.ANY)] * 2,
        scratch_shapes=[
            vmem((snaps, 3, nx, ny, nz), f32),
            vmem((nx, snaps, 3, ny, nz), f32),
            vmem((nx, 2 * snaps + 1, 9, ny, nz), f32),
            vmem((nx, 9, bins + 6, ny, nz), f32),
            vmem((4, 6, bins, planes, ny, nz), f32),
            vmem((3, bins, planes, ny, nz), f32),
            vmem((8, 128), i32),
            vmem((8, 128), i32),
            pltpu.SMEM((8, 128), i32),
            vmem((8, 128), i32),
            pltpu.SMEM((8, 128), i32),
            vmem((8, 128), f32),
            pltpu.SMEM((8, 128), f32),
            dma((1,)),
            dma((3,)),
            dma((2,)),
            dma((nx,)),
            dma((nx,)),
            dma((2 * planes,)),
            dma((2 * planes,)),
            dma((2 + GROUPS,)),
        ],
        compiler_params=pltpu.CompilerParams(
            collective_id=0, has_side_effects=True, vmem_limit_bytes=48 * 1024 * 1024
        ),
        cost_estimate=pl.CostEstimate(flops=60_000_000, bytes_accessed=8_000_000, transcendentals=0),
    )(snapshots, phase_index)


def fits_pairs(mesh, snapshots):
    nrev, nbin = mesh.shape["rev"], mesh.shape["bin"]
    snaps, planes, bins = snapshots.shape[1] // nbin, snapshots.shape[3] // nrev, PHASES // nbin
    whole_tiles = snapshots.shape[4:] == (8, 128)
    return nrev == 2 and nbin >= 3 and planes == 3 and 2 * snaps <= 128 and bins % GROUPS == 0 and bins <= 128 and whole_tiles


def solution(mesh):
    in_specs = (P("rev", "bin", None, None, None, None), P("rev", "bin"))
    out_specs = (P(None, None, "bin", "rev", None, None), P(None, "bin", "rev", None, None))

    def run(snapshots, phase_index):
        body = paired_shards if fits_pairs(mesh, snapshots) else shards
        mapped = jax.shard_map(body, mesh=mesh, in_specs=in_specs, out_specs=out_specs, check_vma=False)
        return mapped(snapshots, phase_index)

    return run
```

```python
import functools

import jax
import jax.numpy as jnp
from jax import lax
from jax.experimental import pallas as pl
from jax.experimental.pallas import tpu as pltpu
from jax.sharding import PartitionSpec as P

PHASES = 256


viscosity = 0.2
stress_pairs = ((0, 0), (0, 1), (0, 2), (1, 1), (1, 2), (2, 2))


def padded_2(cells, sides, width):
    for axis, dim in sides:
        count = lax.axis_size(axis)
        head = lax.slice_in_dim(cells, 0, width, axis=dim)
        tail = lax.slice_in_dim(cells, cells.shape[dim] - width, cells.shape[dim], axis=dim)
        cells = jnp.concatenate(
            [
                lax.ppermute(tail, axis, [(i, (i + 1) % count) for i in range(count)]),
                cells,
                lax.ppermute(head, axis, [((i + 1) % count, i) for i in range(count)]),
            ],
            axis=dim,
        )
    return cells


def pair_index(first, second):
    low, high = (min(first, second), max(first, second))
    return stress_pairs.index((low, high))


def binned(frames, weights):
    vel_x, vel_y, vel_z = (frames[:, 0], frames[:, 1], frames[:, 2])
    stacked = jnp.stack(
        [
            jnp.ones_like(vel_x),
            vel_x,
            vel_y,
            vel_z,
            vel_x * vel_x,
            vel_x * vel_y,
            vel_x * vel_z,
            vel_y * vel_y,
            vel_y * vel_z,
            vel_z * vel_z,
        ],
        axis=1,
    )
    return jnp.einsum("ps,sfxyz->xfpyz", weights, stacked, precision=lax.Precision.HIGHEST)


def first_diff(shifted):
    return (
        0.75 * (shifted(1) - shifted(-1))
        - 0.15 * (shifted(2) - shifted(-2))
        + (shifted(3) - shifted(-3)) / 60.0
    )


def second_diff(shifted, centre):
    return (
        -49.0 / 18.0 * centre
        + 1.5 * (shifted(1) + shifted(-1))
        - 0.15 * (shifted(2) + shifted(-2))
        + (shifted(3) + shifted(-3)) / 90.0
    )


def finish_terms(owned):
    planes, bins_dev = (owned.shape[0], owned.shape[2])
    samples = owned[:, 0]
    velocity = [owned[:, 1 + comp] / samples for comp in range(3)]
    stresses = [
        owned[:, 4 + slot] / samples - velocity[pair[0]] * velocity[pair[1]]
        for slot, pair in enumerate(stress_pairs)
    ]
    fields = jnp.stack(velocity + stresses, axis=1)
    padded = padded_2(fields, (("rev", 0), ("bin", 2)), 3)

    def along(component, dim, centre):
        source = padded[:, component]
        if dim == 0:
            return lambda amount: source[3 + amount : 3 + amount + planes, 3 : 3 + bins_dev]
        if dim == 3:
            return lambda amount: source[3 : 3 + planes, 3 + amount : 3 + amount + bins_dev]
        return lambda amount: jnp.roll(centre, -amount, dim + 1)

    grad_u = [
        [first_diff(along(comp, dim, velocity[comp])) for dim in range(3)] for comp in range(3)
    ]
    unsteady, convect, produce, diffuse = ([], [], [], [])
    for slot, pair in enumerate(stress_pairs):
        first, second = pair
        stress = stresses[slot]
        unsteady.append(first_diff(along(3 + slot, 3, stress)))
        grads = [first_diff(along(3 + slot, dim, stress)) for dim in range(3)]
        convect.append(velocity[0] * grads[0] + velocity[1] * grads[1] + velocity[2] * grads[2])
        summed = jnp.zeros_like(stress)
        for dim in range(3):
            summed = (
                summed
                + stresses[pair_index(first, dim)] * grad_u[second][dim]
                + stresses[pair_index(second, dim)] * grad_u[first][dim]
            )
        produce.append(-summed)
        diffuse.append(
            viscosity
            * (
                second_diff(along(3 + slot, 0, stress), stress)
                + second_diff(along(3 + slot, 1, stress), stress)
                + second_diff(along(3 + slot, 2, stress), stress)
            )
        )
    terms_all = jnp.stack(
        [jnp.stack(unsteady), jnp.stack(convect), jnp.stack(produce), jnp.stack(diffuse)]
    )
    return (
        jnp.transpose(terms_all, (0, 1, 3, 2, 4, 5)),
        jnp.transpose(jnp.stack(velocity), (0, 2, 1, 3, 4)),
    )


def shards(snapshots, phase_index):
    frames = snapshots[0]
    bins_dev = PHASES // lax.axis_size("bin")
    local_bins = phase_index[0] - lax.axis_index("bin") * bins_dev
    exchanged = lax.all_to_all(frames, "rev", split_axis=2, concat_axis=0, tiled=True)
    all_bins = lax.all_gather(local_bins, "rev", axis=0, tiled=True)
    one_hot = (all_bins[None, :] == jnp.arange(bins_dev, dtype=jnp.int32)[:, None]).astype(
        jnp.float32
    )
    owned = binned(exchanged, one_hot)
    return finish_terms(owned)


MESH = pl.DeviceIdType.MESH
DEPTH = 2
GROUPS = 4


def turned(tile, amount, axis):
    size = tile.shape[axis]
    return pltpu.roll(tile, (-amount) % size, axis)


def both_diffs(tile, axis):
    plus = [turned(tile, s, axis) for s in (1, 2, 3)]
    minus = [turned(tile, -s, axis) for s in (1, 2, 3)]
    d1 = 0.75 * (plus[0] - minus[0]) - 0.15 * (plus[1] - minus[1]) + (plus[2] - minus[2]) * (1.0 / 60.0)
    d2 = (
        (-49.0 / 18.0) * tile
        + 1.5 * (plus[0] + minus[0])
        - 0.15 * (plus[1] + minus[1])
        + (plus[2] + minus[2]) * (1.0 / 90.0)
    )
    return d1, d2


diff_one = {1: 0.75, -1: -0.75, 2: -0.15, -2: 0.15, 3: 1.0 / 60.0, -3: -1.0 / 60.0}
diff_two = {0: -49.0 / 18.0, 1: 1.5, -1: 1.5, 2: -0.15, -2: -0.15, 3: 1.0 / 90.0, -3: 1.0 / 90.0}


def ring_weights(weights, at, size):
    row = [[] for _ in range(size)]
    for shift, weight in weights.items():
        row[(at + shift) % size].append(weight)
    return [sum(parts) for parts in row]


def weighted(row, tiles):
    total = None
    for weight, tile in zip(row, tiles):
        if weight != 0.0:
            part = weight * tile
            total = part if total is None else total + part
    return total


def moments(vel):
    return list(vel) + [vel[a] * vel[b] for a, b in stress_pairs]


def ring_kernel(
    sizes, snap, index, held, held_mean, base, late,
    own, peer, heap, fields, idx_in, idx_own, idx_peer, idx_s, tab_v, tab_s, inv_v, inv_s,
    load_sem, small_sem, idx_sem, send_sem, recv_sem, halo_send, halo_recv,
):
    snaps, nx, planes, bins, nbin = sizes
    rev, me = lax.axis_index("rev"), lax.axis_index("bin")
    left, right = lax.rem(me + nbin - 1, nbin), lax.rem(me + 1, nbin)
    other = 1 - rev

    barrier = pltpu.get_barrier_semaphore()
    for target in ((other, me), (rev, left), (rev, right)):
        pl.semaphore_signal(barrier, inc=1, device_id=target, device_id_type=MESH)
    get_index = pltpu.make_async_copy(index, idx_in, load_sem.at[1])
    get_index.start()
    whole = pltpu.make_async_copy(snap.at[0], own, load_sem.at[0])
    idx_own[...] = jnp.full(idx_own.shape, -1, jnp.int32)
    get_index.wait()
    idx_own[0:1, 0:snaps] = idx_in[...] - me * bins
    pl.semaphore_wait(barrier, 3)

    copy_idx = pltpu.make_async_remote_copy(
        src_ref=idx_own, dst_ref=idx_peer, send_sem=idx_sem.at[0], recv_sem=idx_sem.at[1],
        device_id=(other, me), device_id_type=MESH,
    )
    copy_idx.start()
    cut = snaps * 3 // 4
    pieces = [(q, 0, snaps) for q in range(nx - 1)] + [(nx - 1, 0, cut), (nx - 1, cut, snaps)]
    sends = []
    for n, (q, lo, hi) in enumerate(pieces):
        plane = lax.rem(q + planes * other, nx)
        sends.append(
            pltpu.make_async_remote_copy(
                src_ref=snap.at[0, lo:hi, :, plane], dst_ref=peer.at[q, lo:hi],
                send_sem=send_sem.at[n], recv_sem=recv_sem.at[n],
                device_id=(other, me), device_id_type=MESH,
            )
        )
    for n in range(DEPTH):
        sends[n].start()
    whole.start()

    copy_idx.wait()
    lane = lax.broadcasted_iota(jnp.int32, (1, 128), 1)
    row = jnp.where(lane < snaps, idx_own[0:1, :], pltpu.roll(idx_peer[0:1, :], snaps, 1))
    idx_own[1:2, :] = row
    to_s = pltpu.make_async_copy(idx_own, idx_s, small_sem.at[0])
    to_s.start()
    to_s.wait()

    def link(j, carry):
        prev, last, count = carry
        b = idx_s[1, j]
        prev = jnp.where((row == b) & (lane > j), j + 1, prev)
        hit = lane == b
        return prev, jnp.where(hit, j + 1, last), count + jnp.where(hit, 1.0, 0.0)

    zero_i = jnp.zeros((1, 128), jnp.int32)
    prev, last, count = lax.fori_loop(
        0, 2 * snaps, link, (zero_i, zero_i, jnp.zeros((1, 128), jnp.float32))
    )
    tab_v[...] = jnp.zeros(tab_v.shape, jnp.int32)
    tab_v[0:1, :] = prev
    tab_v[1:2, :] = last
    inv_v[...] = jnp.broadcast_to(1.0 / jnp.maximum(count, 1.0), inv_v.shape)
    to_t = pltpu.make_async_copy(tab_v, tab_s, small_sem.at[1])
    to_i = pltpu.make_async_copy(inv_v, inv_s, small_sem.at[2])
    to_t.start()
    to_i.start()
    zero = jnp.zeros(heap.shape[-2:], jnp.float32)
    for q in range(nx):
        for m in range(9):
            heap[q, 0, m] = zero
    to_t.wait()
    to_i.wait()
    whole.wait()

    def add_own(k, carry):
        before = tab_s[0, k]
        for q in range(nx):
            plane = lax.rem(q + planes * rev, nx)
            values = moments([own[k, c, plane] for c in range(3)])
            for m in range(9):
                heap[q, k + 1, m] = heap[q, before, m] + values[m]
        return carry

    lax.fori_loop(0, snaps, add_own, 0)

    def add_peer(q, lo, hi):
        def body(k, carry):
            before = tab_s[0, k + snaps]
            values = moments([peer[q, k, c] for c in range(3)])
            for m in range(9):
                heap[q, k + snaps + 1, m] = heap[q, before, m] + values[m]
            return carry

        lax.fori_loop(lo, hi, body, 0)

    def finish(q):
        def body(p, carry):
            at = tab_s[1, p]
            scale = inv_s[0, p]
            vel = [heap[q, at, c] * scale for c in range(3)]
            stress = [
                heap[q, at, 3 + m] * scale - vel[a] * vel[b] for m, (a, b) in enumerate(stress_pairs)
            ]
            if q == nx - 1:
                for n, tile in enumerate(vel + stress):
                    late[p, n] = tile
            else:
                for n, tile in enumerate(vel + stress):
                    fields[q, n, p + 3] = tile
            if q < planes:
                for c in range(3):
                    held_mean[c, p, q] = vel[c]
                    base[p, c, q] = stress[pair_index(c, 0)]
            return carry

        lax.fori_loop(0, bins, body, 0)

    def in_plane(q):
        def body(p, carry):
            vel = [fields[q, c, p + 3] for c in range(3)]
            stress = [fields[q, 3 + m, p + 3] for m in range(6)]
            grad = []
            for c in range(3):
                grad.append([both_diffs(vel[c], 0)[0], both_diffs(vel[c], 1)[0]])
            for m, (a, b) in enumerate(stress_pairs):
                y1, y2 = both_diffs(stress[m], 0)
                z1, z2 = both_diffs(stress[m], 1)
                held[1, m, p, q] = vel[1] * y1 + vel[2] * z1
                held[3, m, p, q] = y2 + z2
                total = None
                for k in (1, 2):
                    part = stress[pair_index(a, k)] * grad[b][k - 1] + stress[pair_index(b, k)] * grad[a][k - 1]
                    total = part if total is None else total + part
                held[2, m, p, q] = total
            return carry

        lax.fori_loop(0, bins, body, 0)

    halos = []
    for q in range(planes):
        halos.append(
            (
                pltpu.make_async_remote_copy(
                    src_ref=fields.at[q, 3:9, 3:6], dst_ref=fields.at[q, 3:9, bins + 3 : bins + 6],
                    send_sem=halo_send.at[2 * q], recv_sem=halo_recv.at[2 * q],
                    device_id=(rev, left), device_id_type=MESH,
                ),
                pltpu.make_async_remote_copy(
                    src_ref=fields.at[q, 3:9, bins : bins + 3], dst_ref=fields.at[q, 3:9, 0:3],
                    send_sem=halo_send.at[2 * q + 1], recv_sem=halo_recv.at[2 * q + 1],
                    device_id=(rev, right), device_id_type=MESH,
                ),
            )
        )

    def in_phase(q):
        def body(p, carry):
            for m in range(6):
                f = lambda s: fields[q, 3 + m, p + 3 + s]
                held[0, m, p, q] = (
                    0.75 * (f(1) - f(-1)) - 0.15 * (f(2) - f(-2)) + (f(3) - f(-3)) * (1.0 / 60.0)
                )
            return carry

        lax.fori_loop(0, bins, body, 0)

    one = [ring_weights(diff_one, q, nx)[: nx - 1] for q in range(planes)]
    two = [ring_weights(diff_two, q, nx)[: nx - 1] for q in range(planes)]

    def across(p, carry):
        grad = []
        for c in range(3):
            tiles = [fields[q, c, p + 3] for q in range(nx - 1)]
            grad.append([weighted(one[q], tiles) for q in range(planes)])
        for m, (a, b) in enumerate(stress_pairs):
            tiles = [fields[q, 3 + m, p + 3] for q in range(nx - 1)]
            for q in range(planes):
                held[1, m, p, q] = held[1, m, p, q] + fields[q, 0, p + 3] * weighted(one[q], tiles)
                held[3, m, p, q] = viscosity * (held[3, m, p, q] + weighted(two[q], tiles))
                part = (
                    fields[q, 3 + pair_index(a, 0), p + 3] * grad[b][q]
                    + fields[q, 3 + pair_index(b, 0), p + 3] * grad[a][q]
                )
                held[2, m, p, q] = -(held[2, m, p, q] + part)
        return carry

    for n, (q, lo, hi) in enumerate(pieces):
        sends[n].wait()
        if n + DEPTH < len(pieces):
            sends[n + DEPTH].start()
        add_peer(q, lo, hi)
        if hi == snaps:
            finish(q)
        if q < planes:
            for halo in halos[q]:
                halo.start()
            in_plane(q)
        if 1 <= q <= planes:
            for halo in halos[q - 1]:
                halo.wait()
            in_phase(q - 1)
        if q == nx - 2:
            lax.fori_loop(0, bins, across, 0)


def last_kernel(sizes, held, held_mean, base, late, terms, mean, done, out_sem):
    nx, planes, bins = sizes
    outs = [
        pltpu.make_async_copy(held.at[0], terms.at[0], out_sem.at[0]),
        pltpu.make_async_copy(held_mean, mean, out_sem.at[1]),
    ]
    for out in outs:
        out.start()
    one = [ring_weights(diff_one, q, nx)[nx - 1] for q in range(planes)]
    two = [viscosity * ring_weights(diff_two, q, nx)[nx - 1] for q in range(planes)]

    def body(p, carry):
        vel = [late[p, c] for c in range(3)]
        stress = [late[p, 3 + m] for m in range(6)]
        for q in range(planes):
            vel_x = held_mean[0, p, q] * one[q]
            near = [base[p, c, q] * one[q] for c in range(3)]
            for m, (a, b) in enumerate(stress_pairs):
                done[0, m, p, q] = held[1, m, p, q] + vel_x * stress[m]
                done[1, m, p, q] = held[2, m, p, q] - (near[a] * vel[b] + near[b] * vel[a])
                done[2, m, p, q] = held[3, m, p, q] + two[q] * stress[m]
        return carry

    each = bins // GROUPS
    for g in range(GROUPS):
        lax.fori_loop(g * each, (g + 1) * each, body, 0)
        out = pltpu.make_async_copy(
            done.at[:, :, g * each : (g + 1) * each],
            terms.at[1:4, :, g * each : (g + 1) * each],
            out_sem.at[2 + g],
        )
        out.start()
        outs.append(out)
    for out in outs:
        out.wait()


def paired_shards(snapshots, phase_index):
    _, snaps, _, nx, ny, nz = snapshots.shape
    nbin, nrev = lax.axis_size("bin"), lax.axis_size("rev")
    bins, planes = PHASES // nbin, nx // nrev
    f32, i32 = jnp.float32, jnp.int32
    vmem, dma = pltpu.VMEM, pltpu.SemaphoreType.DMA
    anywhere = pl.BlockSpec(memory_space=pl.ANY)
    near = pl.BlockSpec(memory_space=pltpu.VMEM)
    snapshots = pltpu.with_memory_space_constraint(snapshots, pltpu.HBM)
    phase_index = pltpu.with_memory_space_constraint(phase_index, pltpu.HBM)
    parts = pl.pallas_call(
        functools.partial(ring_kernel, (snaps, nx, planes, bins, nbin)),
        out_shape=(
            vmem((4, 6, bins, planes, ny, nz), f32),
            vmem((3, bins, planes, ny, nz), f32),
            vmem((bins, 3, planes, ny, nz), f32),
            vmem((bins, 9, ny, nz), f32),
        ),
        in_specs=[pl.BlockSpec(memory_space=pltpu.HBM)] * 2,
        out_specs=[near] * 4,
        scratch_shapes=[
            vmem((snaps, 3, nx, ny, nz), f32),
            vmem((nx, snaps, 3, ny, nz), f32),
            vmem((nx, 2 * snaps + 1, 9, ny, nz), f32),
            vmem((nx - 1, 9, bins + 6, ny, nz), f32),
            vmem((1, snaps), i32),
            vmem((8, 128), i32),
            vmem((8, 128), i32),
            pltpu.SMEM((8, 128), i32),
            vmem((8, 128), i32),
            pltpu.SMEM((8, 128), i32),
            vmem((8, 128), f32),
            pltpu.SMEM((8, 128), f32),
            dma((2,)),
            dma((3,)),
            dma((2,)),
            dma((nx + 1,)),
            dma((nx + 1,)),
            dma((2 * planes,)),
            dma((2 * planes,)),
        ],
        compiler_params=pltpu.CompilerParams(
            collective_id=0, has_side_effects=True, vmem_limit_bytes=40 * 1024 * 1024
        ),
        cost_estimate=pl.CostEstimate(flops=60_000_000, bytes_accessed=8_000_000, transcendentals=0),
    )(snapshots, phase_index)
    parts = [pltpu.with_memory_space_constraint(part, pltpu.VMEM) for part in parts]
    return pl.pallas_call(
        functools.partial(last_kernel, (nx, planes, bins)),
        out_shape=(
            jax.ShapeDtypeStruct((4, 6, bins, planes, ny, nz), f32),
            jax.ShapeDtypeStruct((3, bins, planes, ny, nz), f32),
        ),
        in_specs=[near] * 4,
        out_specs=[anywhere] * 2,
        scratch_shapes=[vmem((3, 6, bins, planes, ny, nz), f32), dma((2 + GROUPS,))],
        compiler_params=pltpu.CompilerParams(vmem_limit_bytes=16 * 1024 * 1024),
        cost_estimate=pl.CostEstimate(flops=4_000_000, bytes_accessed=8_000_000, transcendentals=0),
    )(*parts)


def fits_pairs(mesh, snapshots):
    nrev, nbin = mesh.shape["rev"], mesh.shape["bin"]
    snaps, planes, bins = snapshots.shape[1] // nbin, snapshots.shape[3] // nrev, PHASES // nbin
    whole_tiles = snapshots.shape[4:] == (8, 128)
    return nrev == 2 and nbin >= 3 and planes == 3 and 2 * snaps <= 128 and bins % GROUPS == 0 and bins <= 128 and whole_tiles


def solution(mesh):
    in_specs = (P("rev", "bin", None, None, None, None), P("rev", "bin"))
    out_specs = (P(None, None, "bin", "rev", None, None), P(None, "bin", "rev", None, None))

    def run(snapshots, phase_index):
        body = paired_shards if fits_pairs(mesh, snapshots) else shards
        mapped = jax.shard_map(body, mesh=mesh, in_specs=in_specs, out_specs=out_specs, check_vma=False)
        return mapped(snapshots, phase_index)

    return run
```

```python
import functools

import jax
import jax.numpy as jnp
from jax import lax
from jax.experimental import pallas as pl
from jax.experimental.pallas import tpu as pltpu
from jax.sharding import PartitionSpec as P

PHASES = 256


viscosity = 0.2
stress_pairs = ((0, 0), (0, 1), (0, 2), (1, 1), (1, 2), (2, 2))


def padded_2(cells, sides, width):
    for axis, dim in sides:
        count = lax.axis_size(axis)
        head = lax.slice_in_dim(cells, 0, width, axis=dim)
        tail = lax.slice_in_dim(cells, cells.shape[dim] - width, cells.shape[dim], axis=dim)
        cells = jnp.concatenate(
            [
                lax.ppermute(tail, axis, [(i, (i + 1) % count) for i in range(count)]),
                cells,
                lax.ppermute(head, axis, [((i + 1) % count, i) for i in range(count)]),
            ],
            axis=dim,
        )
    return cells


def pair_index(first, second):
    low, high = (min(first, second), max(first, second))
    return stress_pairs.index((low, high))


def binned(frames, weights):
    vel_x, vel_y, vel_z = (frames[:, 0], frames[:, 1], frames[:, 2])
    stacked = jnp.stack(
        [
            jnp.ones_like(vel_x),
            vel_x,
            vel_y,
            vel_z,
            vel_x * vel_x,
            vel_x * vel_y,
            vel_x * vel_z,
            vel_y * vel_y,
            vel_y * vel_z,
            vel_z * vel_z,
        ],
        axis=1,
    )
    return jnp.einsum("ps,sfxyz->xfpyz", weights, stacked, precision=lax.Precision.HIGHEST)


def first_diff(shifted):
    return (
        0.75 * (shifted(1) - shifted(-1))
        - 0.15 * (shifted(2) - shifted(-2))
        + (shifted(3) - shifted(-3)) / 60.0
    )


def second_diff(shifted, centre):
    return (
        -49.0 / 18.0 * centre
        + 1.5 * (shifted(1) + shifted(-1))
        - 0.15 * (shifted(2) + shifted(-2))
        + (shifted(3) + shifted(-3)) / 90.0
    )


def finish_terms(owned):
    planes, bins_dev = (owned.shape[0], owned.shape[2])
    samples = owned[:, 0]
    velocity = [owned[:, 1 + comp] / samples for comp in range(3)]
    stresses = [
        owned[:, 4 + slot] / samples - velocity[pair[0]] * velocity[pair[1]]
        for slot, pair in enumerate(stress_pairs)
    ]
    fields = jnp.stack(velocity + stresses, axis=1)
    padded = padded_2(fields, (("rev", 0), ("bin", 2)), 3)

    def along(component, dim, centre):
        source = padded[:, component]
        if dim == 0:
            return lambda amount: source[3 + amount : 3 + amount + planes, 3 : 3 + bins_dev]
        if dim == 3:
            return lambda amount: source[3 : 3 + planes, 3 + amount : 3 + amount + bins_dev]
        return lambda amount: jnp.roll(centre, -amount, dim + 1)

    grad_u = [
        [first_diff(along(comp, dim, velocity[comp])) for dim in range(3)] for comp in range(3)
    ]
    unsteady, convect, produce, diffuse = ([], [], [], [])
    for slot, pair in enumerate(stress_pairs):
        first, second = pair
        stress = stresses[slot]
        unsteady.append(first_diff(along(3 + slot, 3, stress)))
        grads = [first_diff(along(3 + slot, dim, stress)) for dim in range(3)]
        convect.append(velocity[0] * grads[0] + velocity[1] * grads[1] + velocity[2] * grads[2])
        summed = jnp.zeros_like(stress)
        for dim in range(3):
            summed = (
                summed
                + stresses[pair_index(first, dim)] * grad_u[second][dim]
                + stresses[pair_index(second, dim)] * grad_u[first][dim]
            )
        produce.append(-summed)
        diffuse.append(
            viscosity
            * (
                second_diff(along(3 + slot, 0, stress), stress)
                + second_diff(along(3 + slot, 1, stress), stress)
                + second_diff(along(3 + slot, 2, stress), stress)
            )
        )
    terms_all = jnp.stack(
        [jnp.stack(unsteady), jnp.stack(convect), jnp.stack(produce), jnp.stack(diffuse)]
    )
    return (
        jnp.transpose(terms_all, (0, 1, 3, 2, 4, 5)),
        jnp.transpose(jnp.stack(velocity), (0, 2, 1, 3, 4)),
    )


def shards(snapshots, phase_index):
    frames = snapshots[0]
    bins_dev = PHASES // lax.axis_size("bin")
    local_bins = phase_index[0] - lax.axis_index("bin") * bins_dev
    exchanged = lax.all_to_all(frames, "rev", split_axis=2, concat_axis=0, tiled=True)
    all_bins = lax.all_gather(local_bins, "rev", axis=0, tiled=True)
    one_hot = (all_bins[None, :] == jnp.arange(bins_dev, dtype=jnp.int32)[:, None]).astype(
        jnp.float32
    )
    owned = binned(exchanged, one_hot)
    return finish_terms(owned)


MESH = pl.DeviceIdType.MESH
DEPTH = 2
GROUPS = 8
PIECES = 4


def turned(tile, amount, axis):
    size = tile.shape[axis]
    return pltpu.roll(tile, (-amount) % size, axis)


def both_diffs(tile, axis):
    plus = [turned(tile, s, axis) for s in (1, 2, 3)]
    minus = [turned(tile, -s, axis) for s in (1, 2, 3)]
    d1 = 0.75 * (plus[0] - minus[0]) - 0.15 * (plus[1] - minus[1]) + (plus[2] - minus[2]) * (1.0 / 60.0)
    d2 = (
        (-49.0 / 18.0) * tile
        + 1.5 * (plus[0] + minus[0])
        - 0.15 * (plus[1] + minus[1])
        + (plus[2] + minus[2]) * (1.0 / 90.0)
    )
    return d1, d2


diff_one = {1: 0.75, -1: -0.75, 2: -0.15, -2: 0.15, 3: 1.0 / 60.0, -3: -1.0 / 60.0}
diff_two = {0: -49.0 / 18.0, 1: 1.5, -1: 1.5, 2: -0.15, -2: -0.15, 3: 1.0 / 90.0, -3: 1.0 / 90.0}


def ring_weights(weights, at, size):
    row = [[] for _ in range(size)]
    for shift, weight in weights.items():
        row[(at + shift) % size].append(weight)
    return [sum(parts) for parts in row]


def weighted(row, tiles):
    total = None
    for weight, tile in zip(row, tiles):
        if weight != 0.0:
            part = weight * tile
            total = part if total is None else total + part
    return total


def moments(vel):
    return list(vel) + [vel[a] * vel[b] for a, b in stress_pairs]


def ring_kernel(
    sizes, snap, index, held, held_mean, base, late,
    own, peer, heap, fields, idx_in, idx_own, idx_peer, idx_s, tab_v, tab_s, inv_v, inv_s,
    load_sem, small_sem, idx_sem, send_sem, recv_sem, halo_send, halo_recv,
):
    snaps, nx, planes, bins, nbin = sizes
    rev, me = lax.axis_index("rev"), lax.axis_index("bin")
    left, right = lax.rem(me + nbin - 1, nbin), lax.rem(me + 1, nbin)
    other = 1 - rev

    barrier = pltpu.get_barrier_semaphore()
    for target in ((other, me), (rev, left), (rev, right)):
        pl.semaphore_signal(barrier, inc=1, device_id=target, device_id_type=MESH)
    get_index = pltpu.make_async_copy(index, idx_in, load_sem.at[1])
    get_index.start()
    whole = pltpu.make_async_copy(snap.at[0], own, load_sem.at[0])
    idx_own[...] = jnp.full(idx_own.shape, -1, jnp.int32)
    get_index.wait()
    idx_own[0:1, 0:snaps] = idx_in[...] - me * bins
    pl.semaphore_wait(barrier, 3)

    copy_idx = pltpu.make_async_remote_copy(
        src_ref=idx_own, dst_ref=idx_peer, send_sem=idx_sem.at[0], recv_sem=idx_sem.at[1],
        device_id=(other, me), device_id_type=MESH,
    )
    copy_idx.start()
    cut = snaps // PIECES
    pieces = [(q, 0, snaps) for q in range(nx - 1)]
    pieces += [(nx - 1, n * cut, (n + 1) * cut) for n in range(PIECES)]
    sends = []
    for n, (q, lo, hi) in enumerate(pieces):
        plane = lax.rem(q + planes * other, nx)
        sends.append(
            pltpu.make_async_remote_copy(
                src_ref=snap.at[0, lo:hi, :, plane], dst_ref=peer.at[q, lo:hi],
                send_sem=send_sem.at[n], recv_sem=recv_sem.at[n],
                device_id=(other, me), device_id_type=MESH,
            )
        )
    for n in range(DEPTH):
        sends[n].start()
    whole.start()

    copy_idx.wait()
    lane = lax.broadcasted_iota(jnp.int32, (1, 128), 1)
    row = jnp.where(lane < snaps, idx_own[0:1, :], pltpu.roll(idx_peer[0:1, :], snaps, 1))
    idx_own[1:2, :] = row
    to_s = pltpu.make_async_copy(idx_own, idx_s, small_sem.at[0])
    to_s.start()
    to_s.wait()

    def link(j, carry):
        prev, last, count = carry
        b = idx_s[1, j]
        prev = jnp.where((row == b) & (lane > j), j + 1, prev)
        hit = lane == b
        return prev, jnp.where(hit, j + 1, last), count + jnp.where(hit, 1.0, 0.0)

    zero_i = jnp.zeros((1, 128), jnp.int32)
    prev, last, count = lax.fori_loop(
        0, 2 * snaps, link, (zero_i, zero_i, jnp.zeros((1, 128), jnp.float32))
    )
    tab_v[...] = jnp.zeros(tab_v.shape, jnp.int32)
    tab_v[0:1, :] = prev
    tab_v[1:2, :] = last
    inv_v[...] = jnp.broadcast_to(1.0 / jnp.maximum(count, 1.0), inv_v.shape)
    to_t = pltpu.make_async_copy(tab_v, tab_s, small_sem.at[1])
    to_i = pltpu.make_async_copy(inv_v, inv_s, small_sem.at[2])
    to_t.start()
    to_i.start()
    zero = jnp.zeros(heap.shape[-2:], jnp.float32)
    for q in range(nx):
        for m in range(9):
            heap[q, 0, m] = zero
    to_t.wait()
    to_i.wait()
    whole.wait()

    def add_own(k, carry):
        before = tab_s[0, k]
        for q in range(nx):
            plane = lax.rem(q + planes * rev, nx)
            values = moments([own[k, c, plane] for c in range(3)])
            for m in range(9):
                heap[q, k + 1, m] = heap[q, before, m] + values[m]
        return carry

    lax.fori_loop(0, snaps, add_own, 0)

    def add_peer(q, lo, hi):
        def body(k, carry):
            before = tab_s[0, k + snaps]
            values = moments([peer[q, k, c] for c in range(3)])
            for m in range(9):
                heap[q, k + snaps + 1, m] = heap[q, before, m] + values[m]
            return carry

        lax.fori_loop(lo, hi, body, 0, unroll=4)

    def finish(q):
        def body(p, carry):
            at = tab_s[1, p]
            scale = inv_s[0, p]
            vel = [heap[q, at, c] * scale for c in range(3)]
            stress = [
                heap[q, at, 3 + m] * scale - vel[a] * vel[b] for m, (a, b) in enumerate(stress_pairs)
            ]
            if q == nx - 1:
                for n, tile in enumerate(vel + stress):
                    late[p, n] = tile
            else:
                for n, tile in enumerate(vel + stress):
                    fields[q, n, p + 3] = tile
            if q < planes:
                for c in range(3):
                    held_mean[c, p, q] = vel[c]
                    base[p, c, q] = stress[pair_index(c, 0)]
            return carry

        lax.fori_loop(0, bins, body, 0, unroll=4)

    def in_plane(q):
        def body(p, carry):
            vel = [fields[q, c, p + 3] for c in range(3)]
            stress = [fields[q, 3 + m, p + 3] for m in range(6)]
            grad = []
            for c in range(3):
                grad.append([both_diffs(vel[c], 0)[0], both_diffs(vel[c], 1)[0]])
            for m, (a, b) in enumerate(stress_pairs):
                y1, y2 = both_diffs(stress[m], 0)
                z1, z2 = both_diffs(stress[m], 1)
                held[1, m, p, q] = vel[1] * y1 + vel[2] * z1
                held[3, m, p, q] = y2 + z2
                total = None
                for k in (1, 2):
                    part = stress[pair_index(a, k)] * grad[b][k - 1] + stress[pair_index(b, k)] * grad[a][k - 1]
                    total = part if total is None else total + part
                held[2, m, p, q] = total
            return carry

        lax.fori_loop(0, bins, body, 0)

    halos = []
    for q in range(planes):
        halos.append(
            (
                pltpu.make_async_remote_copy(
                    src_ref=fields.at[q, 3:9, 3:6], dst_ref=fields.at[q, 3:9, bins + 3 : bins + 6],
                    send_sem=halo_send.at[2 * q], recv_sem=halo_recv.at[2 * q],
                    device_id=(rev, left), device_id_type=MESH,
                ),
                pltpu.make_async_remote_copy(
                    src_ref=fields.at[q, 3:9, bins : bins + 3], dst_ref=fields.at[q, 3:9, 0:3],
                    send_sem=halo_send.at[2 * q + 1], recv_sem=halo_recv.at[2 * q + 1],
                    device_id=(rev, right), device_id_type=MESH,
                ),
            )
        )

    def in_phase(q):
        def body(p, carry):
            for m in range(6):
                f = lambda s: fields[q, 3 + m, p + 3 + s]
                held[0, m, p, q] = (
                    0.75 * (f(1) - f(-1)) - 0.15 * (f(2) - f(-2)) + (f(3) - f(-3)) * (1.0 / 60.0)
                )
            return carry

        lax.fori_loop(0, bins, body, 0)

    one = [ring_weights(diff_one, q, nx)[: nx - 1] for q in range(planes)]
    two = [ring_weights(diff_two, q, nx)[: nx - 1] for q in range(planes)]

    def across(p, carry):
        grad = []
        for c in range(3):
            tiles = [fields[q, c, p + 3] for q in range(nx - 1)]
            grad.append([weighted(one[q], tiles) for q in range(planes)])
        for m, (a, b) in enumerate(stress_pairs):
            tiles = [fields[q, 3 + m, p + 3] for q in range(nx - 1)]
            for q in range(planes):
                held[1, m, p, q] = held[1, m, p, q] + fields[q, 0, p + 3] * weighted(one[q], tiles)
                held[3, m, p, q] = viscosity * (held[3, m, p, q] + weighted(two[q], tiles))
                part = (
                    fields[q, 3 + pair_index(a, 0), p + 3] * grad[b][q]
                    + fields[q, 3 + pair_index(b, 0), p + 3] * grad[a][q]
                )
                held[2, m, p, q] = -(held[2, m, p, q] + part)
        return carry

    for n, (q, lo, hi) in enumerate(pieces):
        sends[n].wait()
        if n + DEPTH < len(pieces):
            sends[n + DEPTH].start()
        add_peer(q, lo, hi)
        if hi == snaps:
            finish(q)
        if q < planes:
            for halo in halos[q]:
                halo.start()
            in_plane(q)
        if 1 <= q <= planes:
            for halo in halos[q - 1]:
                halo.wait()
            in_phase(q - 1)
        if q == nx - 2:
            lax.fori_loop(0, bins, across, 0)


def last_kernel(sizes, held, held_mean, base, late, terms, mean, done, out_sem):
    nx, planes, bins = sizes
    outs = [
        pltpu.make_async_copy(held.at[0], terms.at[0], out_sem.at[0]),
        pltpu.make_async_copy(held_mean, mean, out_sem.at[1]),
    ]
    for out in outs:
        out.start()
    one = [ring_weights(diff_one, q, nx)[nx - 1] for q in range(planes)]
    two = [viscosity * ring_weights(diff_two, q, nx)[nx - 1] for q in range(planes)]

    def body(p, carry):
        vel = [late[p, c] for c in range(3)]
        stress = [late[p, 3 + m] for m in range(6)]
        for q in range(planes):
            vel_x = held_mean[0, p, q] * one[q]
            near = [base[p, c, q] * one[q] for c in range(3)]
            for m, (a, b) in enumerate(stress_pairs):
                done[0, m, p, q] = held[1, m, p, q] + vel_x * stress[m]
                done[1, m, p, q] = held[2, m, p, q] - (near[a] * vel[b] + near[b] * vel[a])
                done[2, m, p, q] = held[3, m, p, q] + two[q] * stress[m]
        return carry

    each = bins // GROUPS
    for g in range(GROUPS):
        lax.fori_loop(g * each, (g + 1) * each, body, 0, unroll=True)
        out = pltpu.make_async_copy(
            done.at[:, :, g * each : (g + 1) * each],
            terms.at[1:4, :, g * each : (g + 1) * each],
            out_sem.at[2 + g],
        )
        out.start()
        outs.append(out)
    for out in outs:
        out.wait()


def paired_shards(snapshots, phase_index):
    _, snaps, _, nx, ny, nz = snapshots.shape
    nbin, nrev = lax.axis_size("bin"), lax.axis_size("rev")
    bins, planes = PHASES // nbin, nx // nrev
    f32, i32 = jnp.float32, jnp.int32
    vmem, dma = pltpu.VMEM, pltpu.SemaphoreType.DMA
    anywhere = pl.BlockSpec(memory_space=pl.ANY)
    near = pl.BlockSpec(memory_space=pltpu.VMEM)
    snapshots = pltpu.with_memory_space_constraint(snapshots, pltpu.HBM)
    phase_index = pltpu.with_memory_space_constraint(phase_index, pltpu.HBM)
    parts = pl.pallas_call(
        functools.partial(ring_kernel, (snaps, nx, planes, bins, nbin)),
        out_shape=(
            vmem((4, 6, bins, planes, ny, nz), f32),
            vmem((3, bins, planes, ny, nz), f32),
            vmem((bins, 3, planes, ny, nz), f32),
            vmem((bins, 9, ny, nz), f32),
        ),
        in_specs=[pl.BlockSpec(memory_space=pltpu.HBM)] * 2,
        out_specs=[near] * 4,
        scratch_shapes=[
            vmem((snaps, 3, nx, ny, nz), f32),
            vmem((nx, snaps, 3, ny, nz), f32),
            vmem((nx, 2 * snaps + 1, 9, ny, nz), f32),
            vmem((nx - 1, 9, bins + 6, ny, nz), f32),
            vmem((1, snaps), i32),
            vmem((8, 128), i32),
            vmem((8, 128), i32),
            pltpu.SMEM((8, 128), i32),
            vmem((8, 128), i32),
            pltpu.SMEM((8, 128), i32),
            vmem((8, 128), f32),
            pltpu.SMEM((8, 128), f32),
            dma((2,)),
            dma((3,)),
            dma((2,)),
            dma((nx - 1 + PIECES,)),
            dma((nx - 1 + PIECES,)),
            dma((2 * planes,)),
            dma((2 * planes,)),
        ],
        compiler_params=pltpu.CompilerParams(
            collective_id=0, has_side_effects=True, vmem_limit_bytes=40 * 1024 * 1024
        ),
        cost_estimate=pl.CostEstimate(flops=60_000_000, bytes_accessed=8_000_000, transcendentals=0),
    )(snapshots, phase_index)
    parts = [pltpu.with_memory_space_constraint(part, pltpu.VMEM) for part in parts]
    return pl.pallas_call(
        functools.partial(last_kernel, (nx, planes, bins)),
        out_shape=(
            jax.ShapeDtypeStruct((4, 6, bins, planes, ny, nz), f32),
            jax.ShapeDtypeStruct((3, bins, planes, ny, nz), f32),
        ),
        in_specs=[near] * 4,
        out_specs=[anywhere] * 2,
        scratch_shapes=[vmem((3, 6, bins, planes, ny, nz), f32), dma((2 + GROUPS,))],
        compiler_params=pltpu.CompilerParams(vmem_limit_bytes=16 * 1024 * 1024),
        cost_estimate=pl.CostEstimate(flops=4_000_000, bytes_accessed=8_000_000, transcendentals=0),
    )(*parts)


def fits_pairs(mesh, snapshots):
    nrev, nbin = mesh.shape["rev"], mesh.shape["bin"]
    snaps, planes, bins = snapshots.shape[1] // nbin, snapshots.shape[3] // nrev, PHASES // nbin
    whole_tiles = snapshots.shape[4:] == (8, 128)
    return nrev == 2 and nbin >= 3 and planes == 3 and 2 * snaps <= 128 and bins % GROUPS == 0 and snaps % (4 * PIECES) == 0 and bins <= 128 and whole_tiles


def solution(mesh):
    in_specs = (P("rev", "bin", None, None, None, None), P("rev", "bin"))
    out_specs = (P(None, None, "bin", "rev", None, None), P(None, "bin", "rev", None, None))

    def run(snapshots, phase_index):
        body = paired_shards if fits_pairs(mesh, snapshots) else shards
        mapped = jax.shard_map(body, mesh=mesh, in_specs=in_specs, out_specs=out_specs, check_vma=False)
        return mapped(snapshots, phase_index)

    return run
```

```python
import functools

import jax
import jax.numpy as jnp
from jax import lax
from jax.experimental import pallas as pl
from jax.experimental.pallas import tpu as pltpu
from jax.sharding import PartitionSpec as P

PHASES = 256


viscosity = 0.2
stress_pairs = ((0, 0), (0, 1), (0, 2), (1, 1), (1, 2), (2, 2))


def padded_2(cells, sides, width):
    for axis, dim in sides:
        count = lax.axis_size(axis)
        head = lax.slice_in_dim(cells, 0, width, axis=dim)
        tail = lax.slice_in_dim(cells, cells.shape[dim] - width, cells.shape[dim], axis=dim)
        cells = jnp.concatenate(
            [
                lax.ppermute(tail, axis, [(i, (i + 1) % count) for i in range(count)]),
                cells,
                lax.ppermute(head, axis, [((i + 1) % count, i) for i in range(count)]),
            ],
            axis=dim,
        )
    return cells


def pair_index(first, second):
    low, high = (min(first, second), max(first, second))
    return stress_pairs.index((low, high))


def binned(frames, weights):
    vel_x, vel_y, vel_z = (frames[:, 0], frames[:, 1], frames[:, 2])
    stacked = jnp.stack(
        [
            jnp.ones_like(vel_x),
            vel_x,
            vel_y,
            vel_z,
            vel_x * vel_x,
            vel_x * vel_y,
            vel_x * vel_z,
            vel_y * vel_y,
            vel_y * vel_z,
            vel_z * vel_z,
        ],
        axis=1,
    )
    return jnp.einsum("ps,sfxyz->xfpyz", weights, stacked, precision=lax.Precision.HIGHEST)


def first_diff(shifted):
    return (
        0.75 * (shifted(1) - shifted(-1))
        - 0.15 * (shifted(2) - shifted(-2))
        + (shifted(3) - shifted(-3)) / 60.0
    )


def second_diff(shifted, centre):
    return (
        -49.0 / 18.0 * centre
        + 1.5 * (shifted(1) + shifted(-1))
        - 0.15 * (shifted(2) + shifted(-2))
        + (shifted(3) + shifted(-3)) / 90.0
    )


def finish_terms(owned):
    planes, bins_dev = (owned.shape[0], owned.shape[2])
    samples = owned[:, 0]
    velocity = [owned[:, 1 + comp] / samples for comp in range(3)]
    stresses = [
        owned[:, 4 + slot] / samples - velocity[pair[0]] * velocity[pair[1]]
        for slot, pair in enumerate(stress_pairs)
    ]
    fields = jnp.stack(velocity + stresses, axis=1)
    padded = padded_2(fields, (("rev", 0), ("bin", 2)), 3)

    def along(component, dim, centre):
        source = padded[:, component]
        if dim == 0:
            return lambda amount: source[3 + amount : 3 + amount + planes, 3 : 3 + bins_dev]
        if dim == 3:
            return lambda amount: source[3 : 3 + planes, 3 + amount : 3 + amount + bins_dev]
        return lambda amount: jnp.roll(centre, -amount, dim + 1)

    grad_u = [
        [first_diff(along(comp, dim, velocity[comp])) for dim in range(3)] for comp in range(3)
    ]
    unsteady, convect, produce, diffuse = ([], [], [], [])
    for slot, pair in enumerate(stress_pairs):
        first, second = pair
        stress = stresses[slot]
        unsteady.append(first_diff(along(3 + slot, 3, stress)))
        grads = [first_diff(along(3 + slot, dim, stress)) for dim in range(3)]
        convect.append(velocity[0] * grads[0] + velocity[1] * grads[1] + velocity[2] * grads[2])
        summed = jnp.zeros_like(stress)
        for dim in range(3):
            summed = (
                summed
                + stresses[pair_index(first, dim)] * grad_u[second][dim]
                + stresses[pair_index(second, dim)] * grad_u[first][dim]
            )
        produce.append(-summed)
        diffuse.append(
            viscosity
            * (
                second_diff(along(3 + slot, 0, stress), stress)
                + second_diff(along(3 + slot, 1, stress), stress)
                + second_diff(along(3 + slot, 2, stress), stress)
            )
        )
    terms_all = jnp.stack(
        [jnp.stack(unsteady), jnp.stack(convect), jnp.stack(produce), jnp.stack(diffuse)]
    )
    return (
        jnp.transpose(terms_all, (0, 1, 3, 2, 4, 5)),
        jnp.transpose(jnp.stack(velocity), (0, 2, 1, 3, 4)),
    )


def shards(snapshots, phase_index):
    frames = snapshots[0]
    bins_dev = PHASES // lax.axis_size("bin")
    local_bins = phase_index[0] - lax.axis_index("bin") * bins_dev
    exchanged = lax.all_to_all(frames, "rev", split_axis=2, concat_axis=0, tiled=True)
    all_bins = lax.all_gather(local_bins, "rev", axis=0, tiled=True)
    one_hot = (all_bins[None, :] == jnp.arange(bins_dev, dtype=jnp.int32)[:, None]).astype(
        jnp.float32
    )
    owned = binned(exchanged, one_hot)
    return finish_terms(owned)


MESH = pl.DeviceIdType.MESH
DEPTH = 2
GROUPS = 8


def turned(tile, amount, axis):
    size = tile.shape[axis]
    return pltpu.roll(tile, (-amount) % size, axis)


def both_diffs(tile, axis):
    plus = [turned(tile, s, axis) for s in (1, 2, 3)]
    minus = [turned(tile, -s, axis) for s in (1, 2, 3)]
    d1 = 0.75 * (plus[0] - minus[0]) - 0.15 * (plus[1] - minus[1]) + (plus[2] - minus[2]) * (1.0 / 60.0)
    d2 = (
        (-49.0 / 18.0) * tile
        + 1.5 * (plus[0] + minus[0])
        - 0.15 * (plus[1] + minus[1])
        + (plus[2] + minus[2]) * (1.0 / 90.0)
    )
    return d1, d2


diff_one = {1: 0.75, -1: -0.75, 2: -0.15, -2: 0.15, 3: 1.0 / 60.0, -3: -1.0 / 60.0}
diff_two = {0: -49.0 / 18.0, 1: 1.5, -1: 1.5, 2: -0.15, -2: -0.15, 3: 1.0 / 90.0, -3: 1.0 / 90.0}


def ring_weights(weights, at, size):
    row = [[] for _ in range(size)]
    for shift, weight in weights.items():
        row[(at + shift) % size].append(weight)
    return [sum(parts) for parts in row]


def weighted(row, tiles):
    total = None
    for weight, tile in zip(row, tiles):
        if weight != 0.0:
            part = weight * tile
            total = part if total is None else total + part
    return total


def moments(vel):
    return list(vel) + [vel[a] * vel[b] for a, b in stress_pairs]


def ring_kernel(
    sizes, snap, index, held, held_mean, base, late,
    own, peer, heap, fields, idx_in, idx_own, idx_peer, idx_s, tab_v, tab_s, inv_v, inv_s,
    load_sem, small_sem, idx_sem, send_sem, recv_sem, halo_send, halo_recv,
):
    snaps, nx, planes, bins, nbin = sizes
    rev, me = lax.axis_index("rev"), lax.axis_index("bin")
    left, right = lax.rem(me + nbin - 1, nbin), lax.rem(me + 1, nbin)
    other = 1 - rev

    barrier = pltpu.get_barrier_semaphore()
    for target in ((other, me), (rev, left), (rev, right)):
        pl.semaphore_signal(barrier, inc=1, device_id=target, device_id_type=MESH)
    get_index = pltpu.make_async_copy(index, idx_in, load_sem.at[1])
    get_index.start()
    whole = pltpu.make_async_copy(snap.at[0], own, load_sem.at[0])
    idx_own[...] = jnp.full(idx_own.shape, -1, jnp.int32)
    get_index.wait()
    idx_own[0:1, 0:snaps] = idx_in[...] - me * bins
    pl.semaphore_wait(barrier, 3)

    copy_idx = pltpu.make_async_remote_copy(
        src_ref=idx_own, dst_ref=idx_peer, send_sem=idx_sem.at[0], recv_sem=idx_sem.at[1],
        device_id=(other, me), device_id_type=MESH,
    )
    copy_idx.start()
    cut = snaps * 3 // 4
    pieces = [(q, 0, snaps) for q in range(nx - 1)] + [(nx - 1, 0, cut), (nx - 1, cut, snaps)]
    sends = []
    for n, (q, lo, hi) in enumerate(pieces):
        plane = lax.rem(q + planes * other, nx)
        sends.append(
            pltpu.make_async_remote_copy(
                src_ref=snap.at[0, lo:hi, :, plane], dst_ref=peer.at[q, lo:hi],
                send_sem=send_sem.at[n], recv_sem=recv_sem.at[n],
                device_id=(other, me), device_id_type=MESH,
            )
        )
    for n in range(DEPTH):
        sends[n].start()
    whole.start()

    copy_idx.wait()
    lane = lax.broadcasted_iota(jnp.int32, (1, 128), 1)
    row = jnp.where(lane < snaps, idx_own[0:1, :], pltpu.roll(idx_peer[0:1, :], snaps, 1))
    idx_own[1:2, :] = row
    to_s = pltpu.make_async_copy(idx_own, idx_s, small_sem.at[0])
    to_s.start()
    to_s.wait()

    def link(j, carry):
        prev, last, count = carry
        b = idx_s[1, j]
        prev = jnp.where((row == b) & (lane > j), j + 1, prev)
        hit = lane == b
        return prev, jnp.where(hit, j + 1, last), count + jnp.where(hit, 1.0, 0.0)

    zero_i = jnp.zeros((1, 128), jnp.int32)
    prev, last, count = lax.fori_loop(
        0, 2 * snaps, link, (zero_i, zero_i, jnp.zeros((1, 128), jnp.float32))
    )
    tab_v[...] = jnp.zeros(tab_v.shape, jnp.int32)
    tab_v[0:1, :] = prev
    tab_v[1:2, :] = last
    inv_v[...] = jnp.broadcast_to(1.0 / jnp.maximum(count, 1.0), inv_v.shape)
    to_t = pltpu.make_async_copy(tab_v, tab_s, small_sem.at[1])
    to_i = pltpu.make_async_copy(inv_v, inv_s, small_sem.at[2])
    to_t.start()
    to_i.start()
    zero = jnp.zeros(heap.shape[-2:], jnp.float32)
    for q in range(nx):
        for m in range(9):
            heap[q, 0, m] = zero
    to_t.wait()
    to_i.wait()
    whole.wait()

    def add_own(k, carry):
        before = tab_s[0, k]
        for q in range(nx):
            plane = lax.rem(q + planes * rev, nx)
            values = moments([own[k, c, plane] for c in range(3)])
            for m in range(9):
                heap[q, k + 1, m] = heap[q, before, m] + values[m]
        return carry

    lax.fori_loop(0, snaps, add_own, 0)

    def add_peer(q, lo, hi):
        def body(k, carry):
            before = tab_s[0, k + snaps]
            values = moments([peer[q, k, c] for c in range(3)])
            for m in range(9):
                heap[q, k + snaps + 1, m] = heap[q, before, m] + values[m]
            return carry

        lax.fori_loop(lo, hi, body, 0, unroll=4)

    def finish(q):
        def body(p, carry):
            at = tab_s[1, p]
            scale = inv_s[0, p]
            vel = [heap[q, at, c] * scale for c in range(3)]
            stress = [
                heap[q, at, 3 + m] * scale - vel[a] * vel[b] for m, (a, b) in enumerate(stress_pairs)
            ]
            if q == nx - 1:
                for n, tile in enumerate(vel + stress):
                    late[p, n] = tile
            else:
                for n, tile in enumerate(vel + stress):
                    fields[q, n, p + 3] = tile
            if q < planes:
                for c in range(3):
                    held_mean[c, p, q] = vel[c]
                    base[p, c, q] = stress[pair_index(c, 0)]
            return carry

        lax.fori_loop(0, bins, body, 0, unroll=4)

    def in_plane(q):
        def body(p, carry):
            vel = [fields[q, c, p + 3] for c in range(3)]
            stress = [fields[q, 3 + m, p + 3] for m in range(6)]
            grad = []
            for c in range(3):
                grad.append([both_diffs(vel[c], 0)[0], both_diffs(vel[c], 1)[0]])
            for m, (a, b) in enumerate(stress_pairs):
                y1, y2 = both_diffs(stress[m], 0)
                z1, z2 = both_diffs(stress[m], 1)
                held[1, m, p, q] = vel[1] * y1 + vel[2] * z1
                held[3, m, p, q] = y2 + z2
                total = None
                for k in (1, 2):
                    part = stress[pair_index(a, k)] * grad[b][k - 1] + stress[pair_index(b, k)] * grad[a][k - 1]
                    total = part if total is None else total + part
                held[2, m, p, q] = total
            return carry

        lax.fori_loop(0, bins, body, 0)

    halos = []
    for q in range(planes):
        halos.append(
            (
                pltpu.make_async_remote_copy(
                    src_ref=fields.at[q, 3:9, 3:6], dst_ref=fields.at[q, 3:9, bins + 3 : bins + 6],
                    send_sem=halo_send.at[2 * q], recv_sem=halo_recv.at[2 * q],
                    device_id=(rev, left), device_id_type=MESH,
                ),
                pltpu.make_async_remote_copy(
                    src_ref=fields.at[q, 3:9, bins : bins + 3], dst_ref=fields.at[q, 3:9, 0:3],
                    send_sem=halo_send.at[2 * q + 1], recv_sem=halo_recv.at[2 * q + 1],
                    device_id=(rev, right), device_id_type=MESH,
                ),
            )
        )

    def in_phase(q):
        def body(p, carry):
            for m in range(6):
                f = lambda s: fields[q, 3 + m, p + 3 + s]
                held[0, m, p, q] = (
                    0.75 * (f(1) - f(-1)) - 0.15 * (f(2) - f(-2)) + (f(3) - f(-3)) * (1.0 / 60.0)
                )
            return carry

        lax.fori_loop(0, bins, body, 0)

    one = [ring_weights(diff_one, q, nx)[: nx - 1] for q in range(planes)]
    two = [ring_weights(diff_two, q, nx)[: nx - 1] for q in range(planes)]

    def across(p, carry):
        grad = []
        for c in range(3):
            tiles = [fields[q, c, p + 3] for q in range(nx - 1)]
            grad.append([weighted(one[q], tiles) for q in range(planes)])
        for m, (a, b) in enumerate(stress_pairs):
            tiles = [fields[q, 3 + m, p + 3] for q in range(nx - 1)]
            for q in range(planes):
                held[1, m, p, q] = held[1, m, p, q] + fields[q, 0, p + 3] * weighted(one[q], tiles)
                held[3, m, p, q] = viscosity * (held[3, m, p, q] + weighted(two[q], tiles))
                part = (
                    fields[q, 3 + pair_index(a, 0), p + 3] * grad[b][q]
                    + fields[q, 3 + pair_index(b, 0), p + 3] * grad[a][q]
                )
                held[2, m, p, q] = -(held[2, m, p, q] + part)
        return carry

    for n, (q, lo, hi) in enumerate(pieces):
        sends[n].wait()
        if n + DEPTH < len(pieces):
            sends[n + DEPTH].start()
        add_peer(q, lo, hi)
        if hi == snaps:
            finish(q)
        if q < planes:
            for halo in halos[q]:
                halo.start()
            in_plane(q)
        if 1 <= q <= planes:
            for halo in halos[q - 1]:
                halo.wait()
            in_phase(q - 1)
        if q == nx - 2:
            lax.fori_loop(0, bins, across, 0)


def last_kernel(sizes, held, held_mean, base, late, terms, mean, done, out_sem):
    nx, planes, bins = sizes
    outs = [
        pltpu.make_async_copy(held.at[0], terms.at[0], out_sem.at[0]),
        pltpu.make_async_copy(held_mean, mean, out_sem.at[1]),
    ]
    for out in outs:
        out.start()
    one = [ring_weights(diff_one, q, nx)[nx - 1] for q in range(planes)]
    two = [viscosity * ring_weights(diff_two, q, nx)[nx - 1] for q in range(planes)]

    def body(p, carry):
        vel = [late[p, c] for c in range(3)]
        stress = [late[p, 3 + m] for m in range(6)]
        for q in range(planes):
            vel_x = held_mean[0, p, q] * one[q]
            near = [base[p, c, q] * one[q] for c in range(3)]
            for m, (a, b) in enumerate(stress_pairs):
                done[0, m, p, q] = held[1, m, p, q] + vel_x * stress[m]
                done[1, m, p, q] = held[2, m, p, q] - (near[a] * vel[b] + near[b] * vel[a])
                done[2, m, p, q] = held[3, m, p, q] + two[q] * stress[m]
        return carry

    each = bins // GROUPS
    for g in range(GROUPS):
        lax.fori_loop(g * each, (g + 1) * each, body, 0, unroll=True)
        out = pltpu.make_async_copy(
            done.at[:, :, g * each : (g + 1) * each],
            terms.at[1:4, :, g * each : (g + 1) * each],
            out_sem.at[2 + g],
        )
        out.start()
        outs.append(out)
    for out in outs:
        out.wait()


def paired_shards(snapshots, phase_index):
    _, snaps, _, nx, ny, nz = snapshots.shape
    nbin, nrev = lax.axis_size("bin"), lax.axis_size("rev")
    bins, planes = PHASES // nbin, nx // nrev
    f32, i32 = jnp.float32, jnp.int32
    vmem, dma = pltpu.VMEM, pltpu.SemaphoreType.DMA
    anywhere = pl.BlockSpec(memory_space=pl.ANY)
    near = pl.BlockSpec(memory_space=pltpu.VMEM)
    snapshots = pltpu.with_memory_space_constraint(snapshots, pltpu.HBM)
    phase_index = pltpu.with_memory_space_constraint(phase_index, pltpu.HBM)
    parts = pl.pallas_call(
        functools.partial(ring_kernel, (snaps, nx, planes, bins, nbin)),
        out_shape=(
            vmem((4, 6, bins, planes, ny, nz), f32),
            vmem((3, bins, planes, ny, nz), f32),
            vmem((bins, 3, planes, ny, nz), f32),
            vmem((bins, 9, ny, nz), f32),
        ),
        in_specs=[pl.BlockSpec(memory_space=pltpu.HBM)] * 2,
        out_specs=[near] * 4,
        scratch_shapes=[
            vmem((snaps, 3, nx, ny, nz), f32),
            vmem((nx, snaps, 3, ny, nz), f32),
            vmem((nx, 2 * snaps + 1, 9, ny, nz), f32),
            vmem((nx - 1, 9, bins + 6, ny, nz), f32),
            vmem((1, snaps), i32),
            vmem((8, 128), i32),
            vmem((8, 128), i32),
            pltpu.SMEM((8, 128), i32),
            vmem((8, 128), i32),
            pltpu.SMEM((8, 128), i32),
            vmem((8, 128), f32),
            pltpu.SMEM((8, 128), f32),
            dma((2,)),
            dma((3,)),
            dma((2,)),
            dma((nx + 1,)),
            dma((nx + 1,)),
            dma((2 * planes,)),
            dma((2 * planes,)),
        ],
        compiler_params=pltpu.CompilerParams(
            collective_id=0, has_side_effects=True, vmem_limit_bytes=40 * 1024 * 1024
        ),
        cost_estimate=pl.CostEstimate(flops=60_000_000, bytes_accessed=8_000_000, transcendentals=0),
    )(snapshots, phase_index)
    parts = [pltpu.with_memory_space_constraint(part, pltpu.VMEM) for part in parts]
    return pl.pallas_call(
        functools.partial(last_kernel, (nx, planes, bins)),
        out_shape=(
            jax.ShapeDtypeStruct((4, 6, bins, planes, ny, nz), f32),
            jax.ShapeDtypeStruct((3, bins, planes, ny, nz), f32),
        ),
        in_specs=[near] * 4,
        out_specs=[anywhere] * 2,
        scratch_shapes=[vmem((3, 6, bins, planes, ny, nz), f32), dma((2 + GROUPS,))],
        compiler_params=pltpu.CompilerParams(vmem_limit_bytes=16 * 1024 * 1024),
        cost_estimate=pl.CostEstimate(flops=4_000_000, bytes_accessed=8_000_000, transcendentals=0),
    )(*parts)


def fits_pairs(mesh, snapshots):
    nrev, nbin = mesh.shape["rev"], mesh.shape["bin"]
    snaps, planes, bins = snapshots.shape[1] // nbin, snapshots.shape[3] // nrev, PHASES // nbin
    whole_tiles = snapshots.shape[4:] == (8, 128)
    return nrev == 2 and nbin >= 3 and planes == 3 and 2 * snaps <= 128 and bins % GROUPS == 0 and snaps % 16 == 0 and bins <= 128 and whole_tiles


def solution(mesh):
    in_specs = (P("rev", "bin", None, None, None, None), P("rev", "bin"))
    out_specs = (P(None, None, "bin", "rev", None, None), P(None, "bin", "rev", None, None))

    def run(snapshots, phase_index):
        body = paired_shards if fits_pairs(mesh, snapshots) else shards
        mapped = jax.shard_map(body, mesh=mesh, in_specs=in_specs, out_specs=out_specs, check_vma=False)
        return mapped(snapshots, phase_index)

    return run
```
